32 devices in a mesh: group: 4 (over y, x), sub: 8 (over z, core).
Axes of the slice: x: 2, y: 2, z: 4, core: 2. Of those that a mesh axis runs over, the one named last changes fastest.
Arguments:
- points: float32 [3, 262144], P(None, ('group', 'sub')), as said below
- probes: float32 [32, 262144], P(None, ('group', 'sub')), may hold values from -6 to 6
- morton: int32 [262144], P(('group', 'sub')), may hold values from 0 to 8191, as said below
- near_list: int32 [2048, 27], P(('group', 'sub')), may hold values from -1 to 2047, as said below
- leaf_far: int32 [2048, 24], P(('group', 'sub')), may hold values from -1 to 2047, as said below
- box_far: int32 [256, 4], P(('group', 'sub')), may hold values from -1 to 255, as said below
- subtree_far: int32 [32, 4], P(('group', 'sub')), may hold values from -1 to 31, as said below
- leaf_skeleton: float32 [2048, 3, 64], P(('group', 'sub')), as said below
- box_skeleton: float32 [256, 3, 128], P(('group', 'sub')), as said below
- subtree_skeleton: float32 [32, 3, 256], P(('group', 'sub')), as said below
- group_skeleton: float32 [4, 3, 256], replicated, as said below
- leaf_basis: float32 [2048, 64, 128], P(('group', 'sub')), may hold values from -0.5 to 0.5
- leaf_transfer: float32 [2048, 64, 128], P(('group', 'sub')), may hold values from -0.25 to 0.25
- box_transfer: float32 [256, 128, 256], P(('group', 'sub')), may hold values from -0.1875 to 0.1875
- subtree_transfer: float32 [32, 256, 256], P(('group', 'sub')), may hold values from -0.375 to 0.375
Outputs:
- kernel_product: float32 [32, 262144], P(None, ('group', 'sub'))
The draws below stay inside these ranges and needn't reach their ends.
Inputs may be any that keep to these rules, and one draw needn't show every extreme that they name: `morton`: each block of 8192 entries is a permutation of 0 to 8191. `near_list`: row l starts with l, then distinct leaves within 32 of l; -1 marks an empty slot. `leaf_far`: row l holds distinct leaves within 32 of l, none in its near list; -1 marks an empty slot. `box_far`: row b holds distinct other boxes of the same subtree; -1 marks an empty slot. `subtree_far`: row c holds distinct other subtrees of the same group; -1 marks an empty slot. `points`: coordinates in leaf-cell units. `leaf_skeleton`: coordinates in leaf-cell units. `box_skeleton`: coordinates in leaf-cell units. `subtree_skeleton`: coordinates in leaf-cell units. `group_skeleton`: coordinates in leaf-cell units.
All inputs are finite; a program needn't handle non-finite values.
Results may differ from the reference program's by a relative error of at most 0.0003.
Values sent between devices are 32-bit elements; how exact they have to be, the bound alone decides.
A program may use at most 128 MiB of HBM per device.

```python
import math
import jax
import jax.numpy as jnp
from jax import lax

P_SIZE = 128
NV = 32
R0 = 64
R1 = 128
R2 = 256
R3 = 256
CH = 8
NEAR = 27
M0 = 24
M1 = 4
HALO = 32
LEAF_DEV = 64
PTS_DEV = 8192
LEAVES = 2048
NPTS = 262144
BOX1 = 256
BOX2 = 32
GROUP_BOXES = 8
M2 = 4
N_GROUP = 4


leaf_spread = 8.0


def decode_cells(codes):
    coords = []
    for axis_id in range(3):
        cell_bits = jnp.zeros_like(codes)
        for level_id in range(7):
            bit_pos = 3 * level_id + axis_id
            cell_bits = cell_bits | (codes >> bit_pos & 1) << level_id
        coords.append(cell_bits)
    return jnp.stack(coords).astype(jnp.float32)


def shared_points(key):
    first_key, second_key = jax.random.split(jax.random.fold_in(key, 11))
    device_total = NPTS // PTS_DEV
    orders = jax.vmap(lambda subkey: jax.random.permutation(subkey, PTS_DEV))(jax.random.split(first_key, device_total)).astype(jnp.int32)
    columns = (orders + (jnp.arange(device_total, dtype=jnp.int32) * PTS_DEV)[:, None]).reshape(NPTS)
    leaves_of = jnp.arange(NPTS, dtype=jnp.int32) // P_SIZE
    placed = decode_cells(leaves_of) + leaf_spread * jax.random.uniform(second_key, (3, NPTS), jnp.float32)
    points = jnp.zeros((3, NPTS), jnp.float32).at[:, columns].set(placed)
    return (points, orders.reshape(NPTS))


def draw_points(key, part):
    return shared_points(key)[0]


def draw_morton(key, part):
    return shared_points(key)[1]


def shared_lists(key):
    key_pick, key_near, key_far = jax.random.split(jax.random.fold_in(key, 23), 3)
    leaf_ids = jnp.arange(LEAVES, dtype=jnp.int32)
    offset_pool = jnp.concatenate([jnp.arange(-HALO, 0, dtype=jnp.int32), jnp.arange(1, HALO + 1, dtype=jnp.int32)])
    picks = jax.vmap(lambda subkey: jax.random.permutation(subkey, 2 * HALO))(jax.random.split(key_pick, LEAVES)).astype(jnp.int32)
    targets = leaf_ids[:, None] + offset_pool[picks]
    inside = (targets >= 0) & (targets < LEAVES)
    full_row = leaf_ids % LEAF_DEV == LEAF_DEV // 2
    near_counts = jax.random.randint(key_near, (LEAVES,), NEAR // 3, NEAR + 1)
    near_counts = jnp.where(full_row, NEAR, near_counts)
    near_slots = jnp.arange(NEAR - 1, dtype=jnp.int32)
    near_keep = (near_slots[None, :] < near_counts[:, None] - 1) & inside[:, :NEAR - 1]
    near_rest = jnp.where(near_keep, targets[:, :NEAR - 1], -1)
    near_table = jnp.concatenate([leaf_ids[:, None], near_rest], axis=1).astype(jnp.int32)
    far_counts = jax.random.randint(key_far, (LEAVES,), M0 // 3, M0 + 1)
    far_counts = jnp.where(full_row, M0, far_counts)
    far_slots = jnp.arange(M0, dtype=jnp.int32)
    far_keep = (far_slots[None, :] < far_counts[:, None]) & inside[:, NEAR - 1:NEAR - 1 + M0]
    far_table = jnp.where(far_keep, targets[:, NEAR - 1:NEAR - 1 + M0], -1).astype(jnp.int32)
    return (near_table, far_table)


def draw_near_list(key, part):
    return shared_lists(key)[0]


def draw_leaf_far(key, part):
    return shared_lists(key)[1]


def sibling_lists(key, node_count, family, most, fewest):
    key_pick, key_count = jax.random.split(key)
    node_ids = jnp.arange(node_count, dtype=jnp.int32)
    position = node_ids % family
    picks = jax.vmap(lambda subkey: jax.random.permutation(subkey, family - 1))(jax.random.split(key_pick, node_count)).astype(jnp.int32)[:, :most]
    others = picks + (picks >= position[:, None]).astype(jnp.int32)
    targets = (node_ids // family * family)[:, None] + others
    counts = jax.random.randint(key_count, (node_count,), fewest, most + 1)
    counts = jnp.where(position == 0, most, counts)
    slots = jnp.arange(most, dtype=jnp.int32)
    return jnp.where(slots[None, :] < counts[:, None], targets, -1).astype(jnp.int32)


def draw_box_far(key, part):
    return sibling_lists(jax.random.fold_in(key, 37), BOX1, CH, M1, 1)


def draw_subtree_far(key, part):
    return sibling_lists(jax.random.fold_in(key, 41), BOX2, GROUP_BOXES, M2, max(M2 // 2, 1))


def skeleton_points(key, node_count, leaf_span, rank_count, spread):
    key_leaf, key_place = jax.random.split(key)
    leaf_ids = jnp.arange(node_count, dtype=jnp.int32)[:, None] * leaf_span + jax.random.randint(key_leaf, (node_count, rank_count), 0, leaf_span)
    cells = decode_cells(leaf_ids).transpose(1, 0, 2)
    return cells + spread * jax.random.uniform(key_place, (node_count, 3, rank_count), jnp.float32)


def draw_leaf_skeleton(key, part):
    return skeleton_points(jax.random.fold_in(key, 51), LEAVES, 1, R0, leaf_spread)


def draw_box_skeleton(key, part):
    return skeleton_points(jax.random.fold_in(key, 53), BOX1, CH, R1, 1.0)


def draw_subtree_skeleton(key, part):
    return skeleton_points(jax.random.fold_in(key, 57), BOX2, CH * CH, R2, 1.0)


def draw_group_skeleton(key, part):
    return skeleton_points(jax.random.fold_in(key, 59), N_GROUP, LEAVES // N_GROUP, R3, 1.0)


def block_levels(key, dims, cuts, low, high):
    loudness = 1.0
    for dim, blocks in cuts:
        draws = jax.random.uniform(jax.random.fold_in(jax.random.fold_in(key, 6), dim), (blocks,), jnp.float32, low / len(cuts), high / len(cuts))
        loudness = loudness * jnp.repeat(jnp.exp(draws), dims[dim] // blocks).reshape((-1,) + (1,) * (len(dims) - 1 - dim))
    return loudness


def normal_values(rng, extent, width, bound, cuts=(), kind=jnp.bfloat16):
    factor_of = block_levels(rng, extent, cuts, -0.22, 0.18) if cuts else 1.0
    values = jax.random.normal(rng, extent, jnp.float32) * width * factor_of
    return jnp.minimum(jnp.maximum(values, -bound), bound).astype(kind)


def setup_inputs(seed: int = 0) -> dict:
    key_of = jax.random.split(jax.random.key(seed), 16)
    points = draw_points(jax.random.fold_in(key_of[15], 71), 0)
    probes = normal_values(key_of[1], (NV, NPTS), 1.0, 6.0, ((1, 32),), jnp.float32)
    morton = draw_morton(jax.random.fold_in(key_of[15], 71), 0)
    near_list = draw_near_list(jax.random.fold_in(key_of[15], 71), 0)
    leaf_far = draw_leaf_far(jax.random.fold_in(key_of[15], 71), 0)
    box_far = draw_box_far(jax.random.fold_in(key_of[15], 71), 0)
    subtree_far = draw_subtree_far(jax.random.fold_in(key_of[15], 71), 0)
    leaf_skeleton = draw_leaf_skeleton(jax.random.fold_in(key_of[15], 71), 0)
    box_skeleton = draw_box_skeleton(jax.random.fold_in(key_of[15], 71), 0)
    subtree_skeleton = draw_subtree_skeleton(jax.random.fold_in(key_of[15], 71), 0)
    group_skeleton = draw_group_skeleton(jax.random.fold_in(key_of[15], 71), 0)
    leaf_basis = normal_values(key_of[11], (LEAVES, R0, P_SIZE), P_SIZE ** -0.5, 0.5, ((0, 32),), jnp.float32)
    leaf_transfer = normal_values(key_of[12], (LEAVES, R0, R1), (CH * R0) ** -0.5, 0.25, ((0, 32),), jnp.float32)
    box_transfer = normal_values(key_of[13], (BOX1, R1, R2), (CH * R1) ** -0.5, 0.1875, ((0, 32),), jnp.float32)
    subtree_transfer = normal_values(key_of[14], (BOX2, R2, R3), R2 ** -0.5, 0.375, ((0, 32),), jnp.float32)
    return {"points": points, "probes": probes, "morton": morton, "near_list": near_list, "leaf_far": leaf_far, "box_far": box_far, "subtree_far": subtree_far, "leaf_skeleton": leaf_skeleton, "box_skeleton": box_skeleton, "subtree_skeleton": subtree_skeleton, "group_skeleton": group_skeleton, "leaf_basis": leaf_basis, "leaf_transfer": leaf_transfer, "box_transfer": box_transfer, "subtree_transfer": subtree_transfer}


highest = lax.Precision.HIGHEST
matern_rate = math.sqrt(3.0) / 12.0

def matern(source, target):
    squared = None
    for coord_id in range(3):
        offset = source[..., coord_id, :, None] - target[..., coord_id, None, :]
        squared = offset * offset if coord_id == 0 else squared + offset * offset
    radius = jnp.sqrt(squared + 0.0001) * matern_rate
    return (1.0 + radius) * jnp.exp(-radius)

def couple(skeleton, coefficients, partner_ids, factor):
    length = partner_ids.shape[0]

    def block_terms(first_row):
        anchor = lax.dynamic_slice_in_dim(skeleton, first_row, 8, 0)
        entries = lax.dynamic_slice_in_dim(partner_ids, first_row, 8, 0)
        usable = (entries >= 0).astype(skeleton.dtype)
        safe_ids = jnp.maximum(entries, 0)
        kernel_tiles = matern(anchor[:, None], skeleton[safe_ids]) * usable[:, :, None, None]
        return jnp.einsum('bjrs,bjvs->bvr', kernel_tiles, coefficients[safe_ids], precision=highest)
    starts = jnp.arange(length // 8, dtype=jnp.int32) * 8
    blocks = lax.map(block_terms, starts)
    return blocks.reshape((length,) + blocks.shape[2:]) * factor

def reference(points, probes, morton, near_list, leaf_far, box_far, subtree_far, leaf_skeleton, box_skeleton, subtree_skeleton, group_skeleton, leaf_basis, leaf_transfer, box_transfer, subtree_transfer):
    offsets = jnp.arange(NPTS, dtype=jnp.int32) // PTS_DEV * PTS_DEV
    columns = morton.astype(jnp.int32) + offsets
    leaf_points = points[:, columns].reshape(3, LEAVES, P_SIZE).transpose(1, 0, 2)
    leaf_probes = probes[:, columns].reshape(NV, LEAVES, P_SIZE).transpose(1, 0, 2)
    near_field = couple(leaf_points, leaf_probes, near_list, (P_SIZE * NEAR) ** (-0.5))
    coef_leaf = jnp.einsum('lvp,lrp->lvr', leaf_probes, leaf_basis, precision=highest)
    coef_box = jnp.einsum('lvr,lrs->lvs', coef_leaf, leaf_transfer, precision=highest).reshape(BOX1, CH, NV, R1).sum(axis=1)
    coef_subtree = jnp.einsum('bvr,brs->bvs', coef_box, box_transfer, precision=highest).reshape(BOX2, CH, NV, R2).sum(axis=1)
    coef_group = jnp.einsum('cvr,crs->cvs', coef_subtree, subtree_transfer, precision=highest).reshape(N_GROUP, GROUP_BOXES, NV, R3).sum(axis=1)
    local_leaf = couple(leaf_skeleton, coef_leaf, leaf_far, (R0 * M0) ** (-0.5))
    local_box = couple(box_skeleton, coef_box, box_far, (R1 * M1) ** (-0.5))
    local_subtree = couple(subtree_skeleton, coef_subtree, subtree_far, (R2 * M2) ** (-0.5))
    other_mask = 1.0 - jnp.eye(N_GROUP, dtype=group_skeleton.dtype)
    group_tiles = matern(group_skeleton[:, None], group_skeleton[None, :]) * other_mask[:, :, None, None]
    local_group = jnp.einsum('ghrs,hvs->gvr', group_tiles, coef_group, precision=highest) * R3 ** (-0.5)
    down_subtree = local_subtree + jnp.einsum('cvs,crs->cvr', jnp.repeat(local_group, GROUP_BOXES, axis=0), subtree_transfer, precision=highest)
    down_box = local_box + jnp.einsum('bvs,brs->bvr', jnp.repeat(down_subtree, CH, axis=0), box_transfer, precision=highest)
    down_leaf = local_leaf + jnp.einsum('lvs,lrs->lvr', jnp.repeat(down_box, CH, axis=0), leaf_transfer, precision=highest)
    result = near_field + jnp.einsum('lvr,lrp->lvp', down_leaf, leaf_basis, precision=highest)
    ordered = result.transpose(1, 0, 2).reshape(NV, NPTS)
    return jnp.zeros_like(ordered).at[:, columns].set(ordered)
```

```python
import functools
import math

import jax
import jax.numpy as jnp
from jax import lax
from jax.experimental import pallas as pl
from jax.experimental.pallas import tpu as pltpu
from jax.sharding import PartitionSpec as P

P_SIZE = 128
CH = 8
HALO = 32
NEAR_STEP = 3
FAR_STEP = 2

highest = lax.Precision.HIGHEST
scale = math.sqrt(3.0) / 12.0 * math.log2(math.e)
soft = 0.0001 * scale * scale
ln2 = math.log(2.0)
f32 = jnp.float32
bf16 = jnp.bfloat16
NT = (((1,), (1,)), ((), ()))


def hdot(a, b):
    return jnp.dot(a, b, precision=highest, preferred_element_type=f32)


def hdot_nt(a, b):
    return lax.dot_general(a, b, NT, precision=highest, preferred_element_type=f32)


def profile(squared):
    squared = jnp.maximum(squared, soft)
    u = squared * lax.rsqrt(squared)
    return (1.0 + ln2 * u) * jnp.exp2(-u)


def split3(v):
    high = v.astype(bf16).astype(f32)
    rest = v - high
    mid = rest.astype(bf16).astype(f32)
    return high, mid, rest - mid


def augmented(x):
    row = lax.broadcasted_iota(jnp.int32, x.shape, 0)
    norm = jnp.sum(x * x, axis=0, keepdims=True)
    source = jnp.where(row < 3, -2.0 * x, jnp.where(row == 3, 1.0, jnp.where(row == 4, norm + soft, 0.0)))
    target = jnp.where(row < 3, x, jnp.where(row == 3, norm, jnp.where(row == 4, 1.0, 0.0)))
    return source, target


def source_rows(v):
    h, m, lo = split3(v)
    return jnp.concatenate([h, m, h, m, lo, h, lo, m], axis=0)


def target_rows(v):
    h, m, lo = split3(v)
    return jnp.concatenate([h, h, m, m, h, lo, m, lo], axis=0)


def coords(block, centre):
    row = lax.broadcasted_iota(jnp.int32, block.shape, 0)
    return jnp.where(row < 3, (block - centre) * scale, 0.0)


def arrange_kernel(
    morton, points, probes, skel, basis, leaf_tr, box_tr, sub_tr,
    geo, q1_out, q2_out, q3_out, rows, pad, got,
):
    leaves = geo.shape[0]
    boxes = q1_out.shape[0]
    pad[...] = jnp.zeros_like(pad)

    def flip(i, c):
        at = pl.ds(pl.multiple_of(i * P_SIZE, P_SIZE), P_SIZE)
        pad[0:32, :] = probes[:, at]
        pad[32:35, :] = points[:, at]
        rows[at, :] = pad[...].T
        return c

    lax.fori_loop(0, leaves, flip, 0)

    def one_leaf(i, j, acc):
        base = i * P_SIZE
        for k in range(P_SIZE):
            got[j, k : k + 1, :] = rows[pl.ds(morton[base + k], 1), :]
        turned = got[j].T
        geo[i, 0:40, :] = turned[0:40]
        geo[i, 35:38, 0:64] = skel[i]
        q0 = hdot_nt(turned[0:32], basis[i])
        geo[i, 40:56, 0:64] = q0[0:16]
        geo[i, 40:56, 64:128] = q0[16:32]
        return acc + hdot(q0, leaf_tr[i])

    def one_box(b, q2):
        def pair(h, acc):
            for j in range(2):
                acc = one_leaf(b * CH + h * 2 + j, j, acc)
            return acc

        q1 = lax.fori_loop(0, CH // 2, pair, jnp.zeros(q1_out.shape[1:], f32))
        q1_out[b] = q1
        return q2 + hdot(q1, box_tr[b])

    q2 = lax.fori_loop(0, boxes, one_box, jnp.zeros(q2_out.shape, f32))
    q2_out[...] = q2
    q3_out[...] = hdot(q2, sub_tr[0])


def couple_kernel(
    near_ids, near_trips, far_ids, far_trips, left, own, right,
    near_out, far_out, src, tgt, xw, src_lo, src_hi, tgt2, qw,
    *, near_width, far_width, near_factor, far_factor,
):
    leaves = own.shape[0]
    total = leaves + 2 * HALO
    first = own[0, 32:40, 0:1]
    centre_pt = first
    centre_sk = jnp.concatenate([first[3:8], first[0:3]], axis=0)

    def prepare(ref, i, at, local):
        block = ref[i, 32:40, :]
        s8, t8 = augmented(coords(block, centre_pt))
        src[at] = source_rows(s8).T.astype(bf16)
        lane = lax.broadcasted_iota(jnp.int32, (8, P_SIZE), 1)
        turned = jnp.concatenate([block[3:8], block[0:3]], axis=0)
        ks8, kt8 = augmented(coords(turned, centre_sk))
        both = source_rows(ks8)
        zero = jnp.zeros_like(both)
        src_lo[at] = jnp.concatenate([both, zero], axis=0).T[0:64].astype(bf16)
        src_hi[at] = jnp.concatenate([zero, both], axis=0).T[0:64].astype(bf16)
        x = ref[i, 0:32, :]
        hi = x.astype(bf16)
        lo = (x - hi.astype(f32)).astype(bf16)
        xw[at, :, 0:128] = jnp.concatenate([hi, lo], axis=0)
        xw[at, :, 128:256] = jnp.concatenate([hi, jnp.zeros_like(lo)], axis=0)
        q = ref[i, 40:56, :]
        qr = pltpu.roll(q, 64, 1)
        low = lax.broadcasted_iota(jnp.int32, (16, P_SIZE), 1) < 64
        twice = jnp.concatenate([jnp.where(low, q, qr), jnp.where(low, qr, q)], axis=0)
        qhi = twice.astype(bf16)
        low2 = lax.broadcasted_iota(jnp.int32, (32, P_SIZE), 1) < 64
        qlo = jnp.where(low2, twice - qhi.astype(f32), 0.0).astype(bf16)
        qw[at] = jnp.concatenate([qhi, qlo], axis=0)
        if local is not None:
            tgt[i] = target_rows(t8).astype(bf16)
            kt8 = jnp.where(lane < 64, kt8, 0.0)
            if local == 1:
                kt8 = pltpu.roll(kt8, 64, 1)
            return target_rows(kt8).astype(bf16)
        return None

    def halo(i, c):
        prepare(left, i, i, None)
        prepare(right, i, i + HALO + leaves, None)
        return c

    lax.fori_loop(0, HALO, halo, 0)

    def middle(p, c):
        for j in range(2):
            i = p * 2 + j
            tgt2[p, j * 64 : j * 64 + 64, :] = prepare(own, i, i + HALO, j)
        return c

    lax.fori_loop(0, leaves // 2, middle, 0)
    src[total] = jnp.zeros(src.shape[1:], bf16)
    xw[total] = jnp.zeros(xw.shape[1:], bf16)
    src_lo[total] = jnp.zeros(src_lo.shape[1:], bf16)
    src_hi[total] = jnp.zeros(src_hi.shape[1:], bf16)
    qw[total] = jnp.zeros(qw.shape[1:], bf16)

    def near_leaf(l, c):
        target = tgt[l]

        def step(t, acc):
            tiles, values = [], []
            for u in range(NEAR_STEP):
                m = near_ids[l * near_width + t * NEAR_STEP + u]
                k = profile(jnp.dot(src[m], target, preferred_element_type=f32))
                hi = k.astype(bf16)
                tiles += [hi, (k - hi.astype(f32)).astype(bf16)]
                values.append(xw[m])
            return acc + jnp.dot(
                jnp.concatenate(values, axis=1),
                jnp.concatenate(tiles, axis=0),
                preferred_element_type=f32,
            )

        acc = lax.fori_loop(0, near_trips[l], step, jnp.zeros((64, P_SIZE), f32))
        near_out[l] = (acc[0:32] + acc[32:64]) * near_factor
        return c

    lax.fori_loop(0, leaves, near_leaf, 0)

    def far_pair(p, c):
        target = tgt2[p]

        def step(t, acc):
            tiles, values = [], []
            for u in range(FAR_STEP):
                at = t * FAR_STEP + u
                a = far_ids[2 * p * far_width + at]
                b = far_ids[(2 * p + 1) * far_width + at]
                k = profile(
                    jnp.dot(src_lo[a] + src_hi[b], target, preferred_element_type=f32)
                )
                hi = k.astype(bf16)
                tiles += [hi, (k - hi.astype(f32)).astype(bf16)]
                values.append(jnp.concatenate([qw[a], qw[b]], axis=0))
            return acc + jnp.dot(
                jnp.concatenate(values, axis=1),
                jnp.concatenate(tiles, axis=0),
                preferred_element_type=f32,
            )

        acc = lax.fori_loop(0, far_trips[p], step, jnp.zeros((128, P_SIZE), f32))
        low = lax.broadcasted_iota(jnp.int32, (32, P_SIZE), 1) < 64
        far_out[p] = (
            jnp.where(low, acc[0:32] + acc[32:64], acc[64:96] + acc[96:128]) * far_factor
        )
        return c

    lax.fori_loop(0, leaves // 2, far_pair, 0)


def centred(block, centre):
    return augmented(coords(block, centre))


def finish_kernel(
    morton, box_far, sub_far, place,
    near, far, q1, gathered, box_skel, group_skel,
    basis, leaf_tr, box_tr, sub_tr,
    out, rows, pad, l1s,
    *, subs, groups, box_width, sub_width, f1, f2, f3,
):
    boxes = q1.shape[0]
    leaves = near.shape[0]
    device, group = place[0], place[1]

    def tile(source8, target8):
        return profile(
            jnp.dot(
                source_rows(source8).T.astype(bf16),
                target_rows(target8).astype(bf16),
                preferred_element_type=f32,
            )
        )

    own = gathered[device, 64:72, :]
    centre = own[:, 0:1]
    target = centred(own, centre)[1]

    def sub_term(j, acc):
        entry = sub_far[j]
        m = jnp.maximum(entry, 0)
        source = centred(gathered[m, 64:72, :], centre)[0]
        term = hdot(gathered[m, 0:32, :], tile(source, target))
        return acc + jnp.where(entry >= 0, term, 0.0)

    z2 = lax.fori_loop(0, sub_width, sub_term, jnp.zeros(gathered[0, 0:32, :].shape, f32))
    g_own = group_skel[group]
    g_centre = g_own[:, 0:1]
    g_target = centred(g_own, g_centre)[1]

    def group_term(h, acc):
        q3 = lax.fori_loop(
            0, subs, lambda s, t: t + gathered[h * subs + s, 32:64, :], jnp.zeros(z2.shape, f32)
        )
        source = centred(group_skel[h], g_centre)[0]
        return acc + jnp.where(h != group, hdot(q3, tile(source, g_target)), 0.0)

    z3 = lax.fori_loop(0, groups, group_term, jnp.zeros(z2.shape, f32))
    l2 = z2 * f2 + hdot_nt(z3 * f3, sub_tr[0])

    def box_level(b, c):
        mine = box_skel[b]
        b_centre = mine[:, 0:1]
        b_target = centred(mine, b_centre)[1]

        def box_term(j, acc):
            entry = box_far[b * box_width + j]
            m = jnp.maximum(entry - device * boxes, 0)
            source = centred(box_skel[m], b_centre)[0]
            return acc + jnp.where(entry >= 0, hdot(q1[m], tile(source, b_target)), 0.0)

        z1 = lax.fori_loop(0, box_width, box_term, jnp.zeros((32, P_SIZE), f32))
        l1s[b] = z1 * f1 + hdot_nt(l2, box_tr[b])
        return c

    lax.fori_loop(0, boxes, box_level, 0)

    pad[...] = jnp.zeros_like(pad)

    def down(p, c):
        l1 = l1s[p // (CH // 2)]
        z = far[p]
        for j in range(2):
            i = 2 * p + j
            l0 = z[:, 64 * j : 64 * j + 64] + hdot_nt(l1, leaf_tr[i])
            y = near[i] + hdot(l0, basis[i])
            pad[j, 0:32, :] = y
            turned = pad[j].T
            pad[2 + j] = turned
            base = i * P_SIZE
            for k in range(P_SIZE):
                rows[pl.ds(morton[base + k], 1), :] = pad[2 + j, k : k + 1, :]
        return c

    lax.fori_loop(0, leaves // 2, down, 0)

    def flip(i, c):
        at = pl.ds(pl.multiple_of(i * P_SIZE, P_SIZE), P_SIZE)
        out[:, at] = rows[at, :].T[0:32]
        return c

    lax.fori_loop(0, leaves, flip, 0)


VMEM = pl.BlockSpec(memory_space=pltpu.VMEM)
SMEM = pl.BlockSpec(memory_space=pltpu.SMEM)
params = pltpu.CompilerParams(vmem_limit_bytes=56 * 2**20)


def slots(ids, base, total, step):
    width = ids.shape[1]
    usable = ids >= 0
    local = jnp.where(usable, ids - base, total)
    more = -width % step
    local = jnp.pad(local, ((0, 0), (0, more)), constant_values=total)
    last = jnp.max(jnp.where(usable, jnp.arange(1, width + 1, dtype=jnp.int32)[None], 0), axis=1)
    return local.reshape(-1), (last + step - 1) // step, width + more


def body(
    points, probes, morton, near_list, leaf_far, box_far, subtree_far,
    leaf_skeleton, box_skeleton, subtree_skeleton, group_skeleton,
    leaf_basis, leaf_transfer, box_transfer, subtree_transfer,
):
    leaves = near_list.shape[0]
    count = points.shape[1]
    nv = probes.shape[0]
    boxes = box_far.shape[0]
    r0, r1 = leaf_basis.shape[1], box_transfer.shape[1]
    r2, r3 = subtree_transfer.shape[1:]
    device = lax.axis_index(("group", "sub"))
    group = lax.axis_index("group")
    subs, groups = lax.axis_size("sub"), lax.axis_size("group")
    total = leaves + 2 * HALO

    geo, q1, q2, q3 = pl.pallas_call(
        arrange_kernel,
        out_shape=(
            jax.ShapeDtypeStruct((leaves, 56, P_SIZE), f32),
            jax.ShapeDtypeStruct((boxes, nv, r1), f32),
            jax.ShapeDtypeStruct((nv, r2), f32),
            jax.ShapeDtypeStruct((nv, r3), f32),
        ),
        in_specs=[SMEM] + [VMEM] * 7,
        out_specs=(VMEM,) * 4,
        scratch_shapes=[
            pltpu.VMEM((count, P_SIZE), f32),
            pltpu.VMEM((P_SIZE, P_SIZE), f32),
            pltpu.VMEM((2, P_SIZE, P_SIZE), f32),
        ],
        compiler_params=params,
        name="arrange",
    )(morton, points, probes, leaf_skeleton, leaf_basis, leaf_transfer, box_transfer, subtree_transfer)

    both = ("group", "sub")
    ends = subs * groups - 1
    left = lax.ppermute(geo[leaves - HALO :], both, [(i, i + 1) for i in range(ends)])
    right = lax.ppermute(geo[:HALO], both, [(i + 1, i) for i in range(ends)])
    packed = jnp.concatenate(
        [q2, q3, subtree_skeleton[0], jnp.zeros((5, r2), f32)], axis=0
    )
    gathered = lax.all_gather(packed, both, axis=0)

    base = device * leaves - HALO
    near_ids, near_trips, near_width = slots(near_list, base, total, NEAR_STEP)
    far_ids, far_trips, far_width = slots(leaf_far, base, total, FAR_STEP)
    far_trips = jnp.max(far_trips.reshape(-1, 2), axis=1)
    near, far = pl.pallas_call(
        functools.partial(
            couple_kernel,
            near_width=near_width,
            far_width=far_width,
            near_factor=(P_SIZE * near_list.shape[1]) ** -0.5,
            far_factor=(r0 * leaf_far.shape[1]) ** -0.5,
        ),
        out_shape=(
            jax.ShapeDtypeStruct((leaves, nv, P_SIZE), f32),
            jax.ShapeDtypeStruct((leaves // 2, nv, P_SIZE), f32),
        ),
        in_specs=[SMEM] * 4 + [VMEM] * 3,
        out_specs=(VMEM,) * 2,
        scratch_shapes=[
            pltpu.VMEM((total + 1, P_SIZE, 64), bf16),
            pltpu.VMEM((leaves, 64, P_SIZE), bf16),
            pltpu.VMEM((total + 1, 64, 256), bf16),
            pltpu.VMEM((total + 1, 64, P_SIZE), bf16),
            pltpu.VMEM((total + 1, 64, P_SIZE), bf16),
            pltpu.VMEM((leaves // 2, P_SIZE, P_SIZE), bf16),
            pltpu.VMEM((total + 1, 64, P_SIZE), bf16),
        ],
        compiler_params=params,
        cost_estimate=pl.CostEstimate(flops=2 * 10**10, bytes_accessed=10**7, transcendentals=5 * 10**7),
        name="couple",
    )(near_ids, near_trips, far_ids, far_trips, left, geo, right)

    pad8 = lambda a: jnp.pad(a, ((0, 0), (0, 5), (0, 0)))
    return pl.pallas_call(
        functools.partial(
            finish_kernel,
            subs=subs,
            groups=groups,
            box_width=box_far.shape[1],
            sub_width=subtree_far.shape[1],
            f1=(r1 * box_far.shape[1]) ** -0.5,
            f2=(r2 * subtree_far.shape[1]) ** -0.5,
            f3=r3**-0.5,
        ),
        out_shape=jax.ShapeDtypeStruct((nv, count), f32),
        in_specs=[SMEM] * 4 + [VMEM] * 10,
        out_specs=VMEM,
        scratch_shapes=[
            pltpu.VMEM((count, P_SIZE), f32),
            pltpu.VMEM((4, P_SIZE, P_SIZE), f32),
            pltpu.VMEM((boxes, nv, P_SIZE), f32),
        ],
        compiler_params=params,
        name="finish",
    )(
        morton, box_far.reshape(-1), subtree_far.reshape(-1),
        jnp.stack([device, group]).astype(jnp.int32),
        near, far, q1, gathered, pad8(box_skeleton), pad8(group_skeleton),
        leaf_basis, leaf_transfer, box_transfer, subtree_transfer,
    )


def solution(mesh):
    two = ("group", "sub")
    placed = (
        (P(None, two),) * 2
        + (P(two),)
        + (P(two, None),) * 4
        + (P(two, None, None),) * 3
        + (P(),)
        + (P(two, None, None),) * 4
    )
    return jax.shard_map(
        body, mesh=mesh, in_specs=placed, out_specs=P(None, two), check_vma=False
    )
```

```python
import functools
import math

import jax
import jax.numpy as jnp
from jax import lax
from jax.experimental import pallas as pl
from jax.experimental.pallas import tpu as pltpu
from jax.sharding import PartitionSpec as P

P_SIZE = 128
CH = 8
HALO = 32
NEAR_STEP = 3
FAR_STEP = 4

highest = lax.Precision.HIGHEST
scale = math.sqrt(3.0) / 12.0 * math.log2(math.e)
soft = 0.0001 * scale * scale
ln2 = math.log(2.0)
f32 = jnp.float32
bf16 = jnp.bfloat16
NT = (((1,), (1,)), ((), ()))


def hdot(a, b):
    return jnp.dot(a, b, precision=highest, preferred_element_type=f32)


def hdot_nt(a, b):
    return lax.dot_general(a, b, NT, precision=highest, preferred_element_type=f32)


def profile(squared):
    squared = jnp.maximum(squared, soft)
    u = squared * lax.rsqrt(squared)
    return (1.0 + ln2 * u) * jnp.exp2(-u)


def split3(v):
    high = v.astype(bf16).astype(f32)
    rest = v - high
    mid = rest.astype(bf16).astype(f32)
    return high, mid, rest - mid


def augmented(x):
    row = lax.broadcasted_iota(jnp.int32, x.shape, 0)
    norm = jnp.sum(x * x, axis=0, keepdims=True)
    source = jnp.where(row < 3, -2.0 * x, jnp.where(row == 3, 1.0, jnp.where(row == 4, norm + soft, 0.0)))
    target = jnp.where(row < 3, x, jnp.where(row == 3, norm, jnp.where(row == 4, 1.0, 0.0)))
    return source, target


def source_rows(v):
    h, m, lo = split3(v)
    return jnp.concatenate([h, m, h, m, lo, h, lo, m], axis=0)


def target_rows(v):
    h, m, lo = split3(v)
    return jnp.concatenate([h, h, m, m, h, lo, m, lo], axis=0)


def coords(block, centre):
    row = lax.broadcasted_iota(jnp.int32, block.shape, 0)
    return jnp.where(row < 3, (block - centre) * scale, 0.0)


def arrange_kernel(
    morton, points, probes, skel, basis, leaf_tr, box_tr, sub_tr,
    geo, q1_out, q2_out, q3_out, rows, pad, got,
):
    leaves = geo.shape[0]
    boxes = q1_out.shape[0]
    pad[...] = jnp.zeros_like(pad)

    def flip(g, c):
        for j in range(4):
            at = pl.ds(pl.multiple_of((4 * g + j) * P_SIZE, P_SIZE), P_SIZE)
            pad[j, 0:32, :] = probes[:, at]
            pad[j, 32:35, :] = points[:, at]
        for j in range(4):
            at = pl.ds(pl.multiple_of((4 * g + j) * P_SIZE, P_SIZE), P_SIZE)
            rows[at, :] = pad[j].T
        return c

    lax.fori_loop(0, leaves // 4, flip, 0)

    def one_box(b, q2):
        for j in range(CH):
            base = (b * CH + j) * P_SIZE
            for k in range(P_SIZE):
                got[j, k : k + 1, :] = rows[pl.ds(morton[base + k], 1), :]
        turned = [got[j].T for j in range(CH)]
        parts = []
        for j in range(CH):
            i = b * CH + j
            geo[i, 0:40, :] = turned[j][0:40]
            geo[i, 35:38, 0:64] = skel[i]
            q0 = hdot_nt(turned[j][0:32], basis[i])
            geo[i, 40:56, 0:64] = q0[0:16]
            geo[i, 40:56, 64:128] = q0[16:32]
            parts.append(q0)
        q1 = jnp.zeros(q1_out.shape[1:], f32)
        for j in range(0, CH, 2):
            two = jnp.concatenate([leaf_tr[b * CH + j], leaf_tr[b * CH + j + 1]], axis=0)
            q1 = q1 + hdot(jnp.concatenate(parts[j : j + 2], axis=1), two)
        q1_out[b] = q1
        return q2 + hdot(q1, box_tr[b])

    q2 = lax.fori_loop(0, boxes, one_box, jnp.zeros(q2_out.shape, f32))
    q2_out[...] = q2
    q3_out[...] = hdot(q2, sub_tr[0])


def couple_kernel(
    near_ids, near_trips, far_ids, far_trips, left, own, right,
    near_out, far_out, src, tgt, xw, src_lo, src_hi, tgt2, qw,
    *, near_width, far_width, near_factor, far_factor,
):
    leaves = own.shape[0]
    total = leaves + 2 * HALO
    first = own[0, 32:40, 0:1]
    centre_pt = first
    centre_sk = jnp.concatenate([first[3:8], first[0:3]], axis=0)

    def prepare(ref, i, at, local):
        block = ref[i, 32:40, :]
        s8, t8 = augmented(coords(block, centre_pt))
        src[at] = source_rows(s8).T.astype(bf16)
        lane = lax.broadcasted_iota(jnp.int32, (8, P_SIZE), 1)
        turned = jnp.concatenate([block[3:8], block[0:3]], axis=0)
        ks8, kt8 = augmented(coords(turned, centre_sk))
        both = source_rows(ks8)
        zero = jnp.zeros_like(both)
        src_lo[at] = jnp.concatenate([both, zero], axis=0).T[0:64].astype(bf16)
        src_hi[at] = jnp.concatenate([zero, both], axis=0).T[0:64].astype(bf16)
        x = ref[i, 0:32, :]
        hi = x.astype(bf16)
        lo = (x - hi.astype(f32)).astype(bf16)
        xw[at, :, 0:128] = jnp.concatenate([hi, lo], axis=0)
        xw[at, :, 128:256] = jnp.concatenate([hi, jnp.zeros_like(lo)], axis=0)
        q = ref[i, 40:56, :]
        qr = pltpu.roll(q, 64, 1)
        low = lax.broadcasted_iota(jnp.int32, (16, P_SIZE), 1) < 64
        twice = jnp.concatenate([jnp.where(low, q, qr), jnp.where(low, qr, q)], axis=0)
        qhi = twice.astype(bf16)
        low2 = lax.broadcasted_iota(jnp.int32, (32, P_SIZE), 1) < 64
        qlo = jnp.where(low2, twice - qhi.astype(f32), 0.0).astype(bf16)
        qw[at] = jnp.concatenate([qhi, qlo], axis=0)
        if local is not None:
            tgt[i] = target_rows(t8).astype(bf16)
            kt8 = jnp.where(lane < 64, kt8, 0.0)
            if local == 1:
                kt8 = pltpu.roll(kt8, 64, 1)
            return target_rows(kt8).astype(bf16)
        return None

    def halo(g, c):
        for j in range(4):
            i = g * 4 + j
            prepare(left, i, i, None)
            prepare(right, i, i + HALO + leaves, None)
        return c

    lax.fori_loop(0, HALO // 4, halo, 0)

    def middle(g, c):
        for j in range(8):
            i = g * 8 + j
            half = j % 2
            tgt2[g * 4 + j // 2, half * 64 : half * 64 + 64, :] = prepare(
                own, i, i + HALO, half
            )
        return c

    lax.fori_loop(0, leaves // 8, middle, 0)
    src[total] = jnp.zeros(src.shape[1:], bf16)
    xw[total] = jnp.zeros(xw.shape[1:], bf16)
    src_lo[total] = jnp.zeros(src_lo.shape[1:], bf16)
    src_hi[total] = jnp.zeros(src_hi.shape[1:], bf16)
    qw[total] = jnp.zeros(qw.shape[1:], bf16)

    def near_leaf(l, c):
        target = tgt[l]

        def steps(count):
            def run():
                tiles, values = [], []
                for u in range(count):
                    m = near_ids[l * near_width + u]
                    k = profile(jnp.dot(src[m], target, preferred_element_type=f32))
                    hi = k.astype(bf16)
                    tiles += [hi, (k - hi.astype(f32)).astype(bf16)]
                    values.append(xw[m])
                return jnp.dot(
                    jnp.concatenate(values, axis=1),
                    jnp.concatenate(tiles, axis=0),
                    preferred_element_type=f32,
                )

            return run

        acc = lax.switch(
            jnp.maximum(near_trips[l], 1) - 1,
            [steps(n) for n in range(NEAR_STEP, near_width + 1, NEAR_STEP)],
        )
        near_out[l] = (acc[0:32] + acc[32:64]) * near_factor
        return c

    lax.fori_loop(0, leaves, near_leaf, 0)

    def far_pair(p, c):
        target = tgt2[p]

        def steps(count):
            def run():
                tiles, values = [], []
                for at in range(count):
                    a = far_ids[2 * p * far_width + at]
                    b = far_ids[(2 * p + 1) * far_width + at]
                    k = profile(
                        jnp.dot(src_lo[a] + src_hi[b], target, preferred_element_type=f32)
                    )
                    hi = k.astype(bf16)
                    tiles += [hi, (k - hi.astype(f32)).astype(bf16)]
                    values.append(jnp.concatenate([qw[a], qw[b]], axis=0))
                return jnp.dot(
                    jnp.concatenate(values, axis=1),
                    jnp.concatenate(tiles, axis=0),
                    preferred_element_type=f32,
                )

            return run

        acc = lax.switch(
            jnp.maximum(far_trips[p], 1) - 1,
            [steps(n) for n in range(FAR_STEP, far_width + 1, FAR_STEP)],
        )
        low = lax.broadcasted_iota(jnp.int32, (32, P_SIZE), 1) < 64
        far_out[p] = (
            jnp.where(low, acc[0:32] + acc[32:64], acc[64:96] + acc[96:128]) * far_factor
        )
        return c

    lax.fori_loop(0, leaves // 2, far_pair, 0)


def centred(block, centre):
    return augmented(coords(block, centre))


def finish_kernel(
    morton, box_far, sub_far, place,
    near, far, q1, gathered, box_skel, group_skel,
    basis, leaf_tr, box_tr, sub_tr,
    out, rows, pad, l1s,
    *, subs, groups, box_width, sub_width, f1, f2, f3,
):
    boxes = q1.shape[0]
    leaves = near.shape[0]
    device, group = place[0], place[1]

    def tile(source8, target8):
        return profile(
            jnp.dot(
                source_rows(source8).T.astype(bf16),
                target_rows(target8).astype(bf16),
                preferred_element_type=f32,
            )
        )

    own = gathered[device, 64:72, :]
    centre = own[:, 0:1]
    target = centred(own, centre)[1]

    def sub_term(j, acc):
        entry = sub_far[j]
        m = jnp.maximum(entry, 0)
        source = centred(gathered[m, 64:72, :], centre)[0]
        term = hdot(gathered[m, 0:32, :], tile(source, target))
        return acc + jnp.where(entry >= 0, term, 0.0)

    many = 4 if sub_width % 4 == 0 else 1

    def sub_terms(g, acc):
        for j in range(many):
            acc = sub_term(g * many + j, acc)
        return acc

    z2 = lax.fori_loop(0, sub_width // many, sub_terms, jnp.zeros(gathered[0, 0:32, :].shape, f32))
    g_own = group_skel[group]
    g_centre = g_own[:, 0:1]
    g_target = centred(g_own, g_centre)[1]

    def group_term(h, acc):
        q3 = lax.fori_loop(
            0, subs, lambda s, t: t + gathered[h * subs + s, 32:64, :], jnp.zeros(z2.shape, f32)
        )
        source = centred(group_skel[h], g_centre)[0]
        return acc + jnp.where(h != group, hdot(q3, tile(source, g_target)), 0.0)

    z3 = jnp.zeros(z2.shape, f32)
    for h in range(groups):
        z3 = group_term(h, z3)
    l2 = z2 * f2 + hdot_nt(z3 * f3, sub_tr[0])

    def box_level(b, c):
        mine = box_skel[b]
        b_centre = mine[:, 0:1]
        b_target = centred(mine, b_centre)[1]

        def box_term(j, acc):
            entry = box_far[b * box_width + j]
            m = jnp.maximum(entry - device * boxes, 0)
            source = centred(box_skel[m], b_centre)[0]
            return acc + jnp.where(entry >= 0, hdot(q1[m], tile(source, b_target)), 0.0)

        z1 = jnp.zeros((32, P_SIZE), f32)
        for j in range(box_width):
            z1 = box_term(j, z1)
        l1s[b] = z1 * f1 + hdot_nt(l2, box_tr[b])
        return c

    def box_pair(g, c):
        for j in range(2):
            box_level(2 * g + j, c)
        return c

    lax.fori_loop(0, boxes // 2, box_pair, 0)

    pad[...] = jnp.zeros_like(pad)

    def down(b, c):
        l1 = l1s[b]
        for j in range(CH):
            i = b * CH + j
            half = 64 * (j % 2)
            l0 = far[b * (CH // 2) + j // 2, :, half : half + 64] + hdot_nt(l1, leaf_tr[i])
            pad[j, 0:32, :] = near[i] + hdot(l0, basis[i])
        for j in range(CH):
            pad[CH + j] = pad[j].T
        for j in range(CH):
            base = (b * CH + j) * P_SIZE
            for k in range(P_SIZE):
                rows[pl.ds(morton[base + k], 1), :] = pad[CH + j, k : k + 1, :]
        return c

    lax.fori_loop(0, boxes, down, 0)

    def flip(g, c):
        for j in range(4):
            at = pl.ds(pl.multiple_of((4 * g + j) * P_SIZE, P_SIZE), P_SIZE)
            out[:, at] = rows[at, :].T[0:32]
        return c

    lax.fori_loop(0, leaves // 4, flip, 0)


VMEM = pl.BlockSpec(memory_space=pltpu.VMEM)
SMEM = pl.BlockSpec(memory_space=pltpu.SMEM)
params = pltpu.CompilerParams(vmem_limit_bytes=56 * 2**20)


def slots(ids, base, total, step):
    width = ids.shape[1]
    usable = ids >= 0
    local = jnp.where(usable, ids - base, total)
    more = -width % step
    local = jnp.pad(local, ((0, 0), (0, more)), constant_values=total)
    last = jnp.max(jnp.where(usable, jnp.arange(1, width + 1, dtype=jnp.int32)[None], 0), axis=1)
    return local.reshape(-1), (last + step - 1) // step, width + more


def body(
    points, probes, morton, near_list, leaf_far, box_far, subtree_far,
    leaf_skeleton, box_skeleton, subtree_skeleton, group_skeleton,
    leaf_basis, leaf_transfer, box_transfer, subtree_transfer,
):
    leaves = near_list.shape[0]
    count = points.shape[1]
    nv = probes.shape[0]
    boxes = box_far.shape[0]
    r0, r1 = leaf_basis.shape[1], box_transfer.shape[1]
    r2, r3 = subtree_transfer.shape[1:]
    device = lax.axis_index(("group", "sub"))
    group = lax.axis_index("group")
    subs, groups = lax.axis_size("sub"), lax.axis_size("group")
    total = leaves + 2 * HALO

    geo, q1, q2, q3 = pl.pallas_call(
        arrange_kernel,
        out_shape=(
            jax.ShapeDtypeStruct((leaves, 56, P_SIZE), f32),
            jax.ShapeDtypeStruct((boxes, nv, r1), f32),
            jax.ShapeDtypeStruct((nv, r2), f32),
            jax.ShapeDtypeStruct((nv, r3), f32),
        ),
        in_specs=[SMEM] + [VMEM] * 7,
        out_specs=(VMEM,) * 4,
        scratch_shapes=[
            pltpu.VMEM((count, P_SIZE), f32),
            pltpu.VMEM((4, P_SIZE, P_SIZE), f32),
            pltpu.VMEM((CH, P_SIZE, P_SIZE), f32),
        ],
        compiler_params=params,
        name="arrange",
    )(morton, points, probes, leaf_skeleton, leaf_basis, leaf_transfer, box_transfer, subtree_transfer)

    both = ("group", "sub")
    ends = subs * groups - 1
    left = lax.ppermute(geo[leaves - HALO :], both, [(i, i + 1) for i in range(ends)])
    right = lax.ppermute(geo[:HALO], both, [(i + 1, i) for i in range(ends)])
    packed = jnp.concatenate(
        [q2, q3, subtree_skeleton[0], jnp.zeros((5, r2), f32)], axis=0
    )
    gathered = lax.all_gather(packed, both, axis=0)

    base = device * leaves - HALO
    near_ids, near_trips, near_width = slots(near_list, base, total, NEAR_STEP)
    far_ids, far_trips, far_width = slots(leaf_far, base, total, FAR_STEP)
    far_trips = jnp.max(far_trips.reshape(-1, 2), axis=1)
    near, far = pl.pallas_call(
        functools.partial(
            couple_kernel,
            near_width=near_width,
            far_width=far_width,
            near_factor=(P_SIZE * near_list.shape[1]) ** -0.5,
            far_factor=(r0 * leaf_far.shape[1]) ** -0.5,
        ),
        out_shape=(
            jax.ShapeDtypeStruct((leaves, nv, P_SIZE), f32),
            jax.ShapeDtypeStruct((leaves // 2, nv, P_SIZE), f32),
        ),
        in_specs=[SMEM] * 4 + [VMEM] * 3,
        out_specs=(VMEM,) * 2,
        scratch_shapes=[
            pltpu.VMEM((total + 1, P_SIZE, 64), bf16),
            pltpu.VMEM((leaves, 64, P_SIZE), bf16),
            pltpu.VMEM((total + 1, 64, 256), bf16),
            pltpu.VMEM((total + 1, 64, P_SIZE), bf16),
            pltpu.VMEM((total + 1, 64, P_SIZE), bf16),
            pltpu.VMEM((leaves // 2, P_SIZE, P_SIZE), bf16),
            pltpu.VMEM((total + 1, 64, P_SIZE), bf16),
        ],
        compiler_params=params,
        cost_estimate=pl.CostEstimate(flops=2 * 10**10, bytes_accessed=10**7, transcendentals=5 * 10**7),
        name="couple",
    )(near_ids, near_trips, far_ids, far_trips, left, geo, right)

    pad8 = lambda a: jnp.pad(a, ((0, 0), (0, 5), (0, 0)))
    return pl.pallas_call(
        functools.partial(
            finish_kernel,
            subs=subs,
            groups=groups,
            box_width=box_far.shape[1],
            sub_width=subtree_far.shape[1],
            f1=(r1 * box_far.shape[1]) ** -0.5,
            f2=(r2 * subtree_far.shape[1]) ** -0.5,
            f3=r3**-0.5,
        ),
        out_shape=jax.ShapeDtypeStruct((nv, count), f32),
        in_specs=[SMEM] * 4 + [VMEM] * 10,
        out_specs=VMEM,
        scratch_shapes=[
            pltpu.VMEM((count, P_SIZE), f32),
            pltpu.VMEM((2 * CH, P_SIZE, P_SIZE), f32),
            pltpu.VMEM((boxes, nv, P_SIZE), f32),
        ],
        compiler_params=params,
        name="finish",
    )(
        morton, box_far.reshape(-1), subtree_far.reshape(-1),
        jnp.stack([device, group]).astype(jnp.int32),
        near, far, q1, gathered, pad8(box_skeleton), pad8(group_skeleton),
        leaf_basis, leaf_transfer, box_transfer, subtree_transfer,
    )


def solution(mesh):
    two = ("group", "sub")
    placed = (
        (P(None, two),) * 2
        + (P(two),)
        + (P(two, None),) * 4
        + (P(two, None, None),) * 3
        + (P(),)
        + (P(two, None, None),) * 4
    )
    return jax.shard_map(
        body, mesh=mesh, in_specs=placed, out_specs=P(None, two), check_vma=False
    )
```
